32 devices in a mesh: seq: 8 (over z, y), tensor: 2 (over x), enc: 2 (over core).
Axes of the slice: x: 2, y: 2, z: 4, core: 2. Of those that a mesh axis runs over, the one named last changes fastest.
Arguments:
- neighbour_rows: bfloat16 [8192, 1024], P('seq'), may hold values from -17 to 17
- norm_gain: float32 [1024], replicated, may hold values from 0.1 to 1.9
- up_weight: bfloat16 [1024, 4096], P(None, ('tensor', 'enc')), may hold values from -0.1875 to 0.1875
- down_weight: bfloat16 [4096, 1024], P(('tensor', 'enc')), may hold values from -0.09375 to 0.09375
- final_gain: float32 [1024], replicated, may hold values from 0.1 to 1.9
- key_weight: bfloat16 [1024, 4096], P(None, ('tensor', 'enc')), may hold values from -0.1875 to 0.1875
- value_weight: bfloat16 [1024, 4096], P(None, ('tensor', 'enc')), may hold values from -0.1875 to 0.1875
- queries: bfloat16 [8192, 4096], P('seq', ('tensor', 'enc')), may hold values from -170 to 170
- block_lists: int32 [128, 2], P('seq'), may hold values from 0 to 63, as said below
- live_counts: int32 [128], P('seq'), may hold values from 1 to 2
Outputs:
- attended: bfloat16 [8192, 4096], P('seq', ('tensor', 'enc'))
The draws below stay inside these ranges and needn't reach their ends.
Inputs may be any that keep to these rules, and one draw needn't show every extreme that they name: `block_lists`: block b of the pool lies on the device of index b // 8 along seq. The two entries of a span name blocks of two different devices. Among all list entries of one device's spans (those beyond a span's count included) at most 4 name blocks of any one device, and in every draw some device's entries reach 4 for some device.
All inputs are finite; a program needn't handle non-finite values.
Results may differ from the reference program's by a relative error of at most 0.019.
The reference program's roundings to bfloat16 on the way (of `normed`, `hidden`, `final_rows`, `key_rows`, `value_rows` and `rounded`) count: a program that leaves them out, or rounds other values in their place, can miss the bound.
Values may be sent and summed in bfloat16 or wider, within the bound.
A program may use at most 128 MiB of HBM per device.

```python
import math
import jax
import jax.numpy as jnp
from jax import lax

DE = 1024
FFE = 4096
H = 32
DH = 128
NB = 128
CL = 64
KMAX = 2
C_DEV = 16
B_DEV = 8
SPANS = 128
POOL = 64
TOKENS = 8192
POOL_ROWS = 8192
N_SEQ = 8


def draw_neighbour_rows(key, part):
    first = jax.random.fold_in(key, 0)
    array_shape = (POOL_ROWS, DE)
    return jnp.clip(jax.random.normal(first, array_shape, jnp.float32), -6.0, 6.0).astype(jnp.bfloat16)


def draw_queries(key, part):
    first = jax.random.fold_in(key, 0)
    array_shape = (TOKENS, H * DH)
    return jnp.clip(jax.random.normal(first, array_shape, jnp.float32), -6.0, 6.0).astype(jnp.bfloat16)


def draw_block_lists(key, part):
    devices = SPANS // C_DEV
    need_count = C_DEV * KMAX
    key_list = jax.random.split(jax.random.fold_in(key, 7), devices)
    orders = jax.vmap(lambda single: jax.random.permutation(single, devices))(key_list)
    position = jnp.arange(need_count) % devices
    owners = orders[:, position]
    first_pick = jax.random.randint(jax.random.fold_in(key, 11), (devices, need_count), 0, B_DEV)
    second_pick = jax.random.randint(jax.random.fold_in(key, 13), (devices, need_count), 0, B_DEV)
    local_index = jnp.minimum(first_pick, second_pick)
    return (owners * B_DEV + local_index).reshape(SPANS, KMAX).astype(jnp.int32)


def set_ends(entries, key, smallest, top_value):
    longest = entries.shape.index(max(entries.shape))
    spots = []
    for shift in (0, 1):
        where = [jax.random.randint(jax.random.fold_in(key, axis), (), 0, length) for axis, length in enumerate(entries.shape)]
        where[longest] = (where[longest] + shift) % entries.shape[longest]
        spots.append(tuple(where))
    return entries.at[spots[0]].set(smallest).at[spots[1]].set(top_value)


def block_levels(own_key, extent, shards, least, largest):
    level = 1.0
    for axis_at, parts in shards:
        heights = jax.random.uniform(jax.random.fold_in(jax.random.fold_in(own_key, 6), axis_at), (parts,), jnp.float32, least / len(shards), largest / len(shards))
        level = level * jnp.repeat(jnp.exp(heights), extent[axis_at] // parts).reshape((-1,) + (1,) * (len(extent) - 1 - axis_at))
    return level


def centred(rng, shape, width, reach, pieces=(), dtype=jnp.bfloat16):
    loudness = block_levels(rng, shape, pieces, -0.22, 0.18) if pieces else 1.0
    values = jax.random.normal(rng, shape, jnp.float32) * width * loudness
    return jnp.minimum(jnp.maximum(values, -reach), reach).astype(dtype)


def setup_inputs(seed: int = 0) -> dict:
    key_of = jax.random.split(jax.random.key(seed), 11)
    return {
        "neighbour_rows": draw_neighbour_rows(jax.random.fold_in(key_of[10], 71), 0),
        "norm_gain": jnp.clip(1.0 + 0.18 * jax.random.normal(key_of[1], (DE,), jnp.float32), 0.1, 1.9),
        "up_weight": centred(key_of[2], (DE, FFE), DE ** -0.5, 0.1875, ((1, 4),)),
        "down_weight": centred(key_of[3], (FFE, DE), FFE ** -0.5, 0.09375, ((0, 4),)),
        "final_gain": jnp.clip(1.0 + 0.18 * jax.random.normal(key_of[4], (DE,), jnp.float32), 0.1, 1.9),
        "key_weight": centred(key_of[5], (DE, H * DH), DE ** -0.5, 0.1875, ((1, 4),)),
        "value_weight": centred(key_of[6], (DE, H * DH), DE ** -0.5, 0.1875, ((1, 4),)),
        "queries": draw_queries(jax.random.fold_in(key_of[10], 71), 0),
        "block_lists": draw_block_lists(jax.random.fold_in(key_of[10], 71), 0),
        "live_counts": set_ends(jax.random.randint(key_of[9], (SPANS,), 1, KMAX + 1), jax.random.fold_in(key_of[9], 1), 1, KMAX).astype(jnp.int32),
    }


def rms_scale(rows, gain):
    mean_square = lax.optimization_barrier(jnp.mean(rows * rows, axis=-1, keepdims=True))
    return rows * lax.rsqrt(mean_square + 1e-06) * gain

def reference(neighbour_rows, norm_gain, up_weight, down_weight, final_gain, key_weight, value_weight, queries, block_lists, live_counts):

    def encode(rows):
        widened = rows.astype(jnp.float32)
        normed = rms_scale(widened, norm_gain).astype(jnp.bfloat16)
        hidden = jax.nn.gelu(jnp.dot(normed, up_weight, preferred_element_type=jnp.float32)).astype(jnp.bfloat16)
        encoded = widened + jnp.dot(hidden, down_weight, preferred_element_type=jnp.float32)
        final_rows = rms_scale(encoded, final_gain).astype(jnp.bfloat16)
        key_part = jnp.dot(final_rows, key_weight, preferred_element_type=jnp.float32).astype(jnp.bfloat16)
        value_part = jnp.dot(final_rows, value_weight, preferred_element_type=jnp.float32).astype(jnp.bfloat16)
        return (key_part, value_part)
    grouped = neighbour_rows.reshape(N_SEQ, B_DEV * NB, DE)
    key_rows, value_rows = lax.map(encode, grouped)
    key_blocks = key_rows.reshape(POOL, NB, H * DH)
    value_blocks = value_rows.reshape(POOL, NB, H * DH)

    def attend(operands):
        query_rows, lists, counts = operands
        query_tiles = query_rows.astype(jnp.float32).reshape(C_DEV, CL, H, DH)
        flat_lists = lists.reshape(C_DEV * KMAX).astype(jnp.int32)
        key_tiles = jnp.take(key_blocks, flat_lists, axis=0).astype(jnp.float32).reshape(C_DEV, KMAX * NB, H, DH)
        value_tiles = jnp.take(value_blocks, flat_lists, axis=0).astype(jnp.float32).reshape(C_DEV, KMAX * NB, H, DH)
        scores = jnp.einsum('cqhd,ckhd->chqk', query_tiles, key_tiles) / math.sqrt(DH)
        live_mask = jnp.arange(KMAX)[None, :] < counts[:, None]
        key_mask = jnp.repeat(live_mask, NB, axis=1)
        scores = jnp.where(key_mask[:, None, None, :], scores, -1e+30)
        highest = lax.optimization_barrier(jnp.max(scores, axis=-1, keepdims=True))
        weights = jnp.exp(scores - highest)
        row_total = lax.optimization_barrier(jnp.sum(weights, axis=-1))
        rounded = lax.optimization_barrier(weights.astype(jnp.bfloat16)).astype(jnp.float32)
        summed = jnp.einsum('chqk,ckhd->cqhd', rounded, value_tiles)
        result = summed / jnp.transpose(row_total, (0, 2, 1))[..., None]
        return result.reshape(C_DEV * CL, H * DH).astype(jnp.bfloat16)
    attended = lax.map(attend, (queries.reshape(N_SEQ, C_DEV * CL, H * DH), block_lists.reshape(N_SEQ, C_DEV, KMAX), live_counts.reshape(N_SEQ, C_DEV)))
    return attended.reshape(TOKENS, H * DH)
```

```python
import functools
import math

import jax
import jax.numpy as jnp
from jax import lax
from jax.experimental import pallas as pl
from jax.experimental.pallas import tpu as pltpu
from jax.sharding import PartitionSpec as P

DH = 128
NB = 128
CL = 64
KMAX = 2
GROUP = ("tensor", "enc")


def rms_scale(rows, gain):
    mean_square = jnp.mean(rows * rows, axis=-1, keepdims=True)
    return rows * lax.rsqrt(mean_square + 1e-06) * gain


def need_ranks(owners):
    need_count = owners.shape[-1]
    order_index = jnp.arange(need_count)
    same_owner = owners[..., :, None] == owners[..., None, :]
    earlier = order_index[None, :] < order_index[:, None]
    return jnp.sum(jnp.logical_and(same_owner, earlier), axis=-1)


def attend_kernel(heads, slots, live, q_ref, k0_ref, k1_ref, v0_ref, v1_ref, o_ref):
    span = pl.program_id(0)
    both = live[span] > 1
    width = heads * DH
    k0 = k0_ref[...].reshape(NB, width)
    k1 = k1_ref[...].reshape(NB, width)
    v0 = v0_ref[...].reshape(NB, width)
    v1 = v1_ref[...].reshape(NB, width)
    contract = (((1,), (1,)), ((), ()))
    for head in range(heads):
        cols = slice(head * DH, (head + 1) * DH)
        q = q_ref[:, cols]
        s0 = lax.dot_general(q, k0[:, cols], contract, preferred_element_type=jnp.float32)
        s1 = lax.dot_general(q, k1[:, cols], contract, preferred_element_type=jnp.float32)
        s0 = s0 / math.sqrt(DH)
        s1 = jnp.where(both, s1 / math.sqrt(DH), -1e30)
        highest = jnp.max(jnp.maximum(s0, s1), axis=-1, keepdims=True)
        w0 = jnp.exp(s0 - highest)
        w1 = jnp.exp(s1 - highest)
        total = jnp.sum(w0 + w1, axis=-1, keepdims=True)
        summed = jnp.dot(
            w0.astype(jnp.bfloat16), v0[:, cols], preferred_element_type=jnp.float32
        ) + jnp.dot(w1.astype(jnp.bfloat16), v1[:, cols], preferred_element_type=jnp.float32)
        o_ref[:, cols] = (summed / total).astype(o_ref.dtype)


def attend(queries, keys, values, slots, live):
    parts, _, rows, width = keys.shape
    spans = live.shape[0]

    def block(entry):
        return pl.BlockSpec(
            (parts, 1, rows, width), lambda c, slots, live: (0, slots[c * KMAX + entry], 0, 0)
        )

    rows_of = pl.BlockSpec((CL, width), lambda c, slots, live: (c, 0))
    return pl.pallas_call(
        functools.partial(attend_kernel, width // DH),
        out_shape=jax.ShapeDtypeStruct(queries.shape, jnp.bfloat16),
        grid_spec=pltpu.PrefetchScalarGridSpec(
            num_scalar_prefetch=2,
            grid=(spans,),
            in_specs=[rows_of, block(0), block(1), block(0), block(1)],
            out_specs=rows_of,
        ),
        compiler_params=pltpu.CompilerParams(vmem_limit_bytes=32 * 2**20),
    )(slots, live, queries, keys, keys, values, values)


def shards(
    neighbour_rows,
    norm_gain,
    up_weight,
    down_weight,
    final_gain,
    key_weight,
    value_weight,
    queries,
    block_lists,
    live_counts,
):
    features = neighbour_rows.shape[1]
    blocks = neighbour_rows.shape[0] // NB
    group = lax.axis_size("tensor") * lax.axis_size("enc")
    part = NB // group
    seq_count = lax.axis_size("seq")
    span_count = live_counts.shape[0]
    need_count = span_count * KMAX
    capacity = (need_count + seq_count - 1) // seq_count

    flat_lists = block_lists.reshape(need_count)
    owners = flat_lists // blocks
    slot_index = owners * capacity + need_ranks(owners)
    every_list = lax.all_gather(block_lists, "seq", axis=0, tiled=True)
    every_flat = every_list.reshape(seq_count, need_count)
    every_owner = every_flat // blocks
    every_rank = need_ranks(every_owner)
    position = lax.axis_index("seq")
    slot_match = jnp.logical_and(
        every_owner[:, :, None] == position,
        every_rank[:, :, None] == jnp.arange(capacity)[None, None, :],
    )
    local_index = every_flat % blocks
    picked = jnp.sum(jnp.where(slot_match, local_index[:, :, None], 0), axis=1).reshape(-1)
    chosen = (picked[:, None] == jnp.arange(blocks)[None, :]).astype(jnp.bfloat16)

    spread = jnp.transpose(neighbour_rows.reshape(blocks, group, part, features), (1, 0, 2, 3))
    widened = spread.reshape(group * blocks * part, features).astype(jnp.float32)
    normed = rms_scale(widened, norm_gain).astype(jnp.bfloat16)
    hidden = jax.nn.gelu(jnp.dot(normed, up_weight, preferred_element_type=jnp.float32)).astype(
        jnp.bfloat16
    )
    partial_sum = jnp.dot(hidden, down_weight, preferred_element_type=jnp.float32)
    summed = lax.psum_scatter(partial_sum, GROUP, scatter_dimension=0, tiled=True)
    me = lax.axis_index("tensor") * lax.axis_size("enc") + lax.axis_index("enc")
    own = lax.dynamic_index_in_dim(spread, me, 0, keepdims=False)
    encoded = own.reshape(blocks * part, features).astype(jnp.float32) + summed
    final_rows = rms_scale(encoded, final_gain).astype(jnp.bfloat16)
    outgoing = jnp.dot(
        chosen,
        final_rows.reshape(blocks, part * features),
        preferred_element_type=jnp.float32,
    ).astype(jnp.bfloat16)
    outgoing = outgoing.reshape(seq_count, capacity * part, features)
    incoming = lax.all_to_all(outgoing, "seq", split_axis=0, concat_axis=0, tiled=True)
    gathered = lax.all_gather(incoming, GROUP, axis=0, tiled=True)
    gathered = gathered.reshape(-1, features)
    shape = (group, seq_count * capacity, part, key_weight.shape[1])
    keys = jnp.dot(gathered, key_weight, preferred_element_type=jnp.float32).astype(jnp.bfloat16)
    values = jnp.dot(gathered, value_weight, preferred_element_type=jnp.float32).astype(
        jnp.bfloat16
    )
    return attend(queries, keys.reshape(shape), values.reshape(shape), slot_index, live_counts)


def solution(mesh):
    placed = (
        P("seq", None),
        P(),
        P(None, GROUP),
        P(GROUP, None),
        P(),
        P(None, GROUP),
        P(None, GROUP),
        P("seq", GROUP),
        P("seq", None),
        P("seq"),
    )
    return jax.shard_map(
        shards, mesh=mesh, in_specs=placed, out_specs=P("seq", GROUP), check_vma=False
    )
```

```python
import functools
import math

import jax
import jax.numpy as jnp
from jax import lax
from jax.experimental import pallas as pl
from jax.experimental.pallas import tpu as pltpu
from jax.sharding import PartitionSpec as P

DH = 128
NB = 128
CL = 64
KMAX = 2
GROUP = ("tensor", "enc")


def rms_scale(rows, gain):
    mean_square = jnp.mean(rows * rows, axis=-1, keepdims=True)
    return rows * lax.rsqrt(mean_square + 1e-06) * gain


def need_ranks(owners):
    need_count = owners.shape[-1]
    order_index = jnp.arange(need_count)
    same_owner = owners[..., :, None] == owners[..., None, :]
    earlier = order_index[None, :] < order_index[:, None]
    return jnp.sum(jnp.logical_and(same_owner, earlier), axis=-1)


def attend_kernel(heads, slots, live, q_ref, k0_ref, k1_ref, v0_ref, v1_ref, o_ref):
    span = pl.program_id(0)
    width = heads * DH
    k0 = k0_ref[...].reshape(NB, width)
    k1 = k1_ref[...].reshape(NB, width)
    v0 = v0_ref[...].reshape(NB, width)
    v1 = v1_ref[...].reshape(NB, width)
    contract = (((1,), (1,)), ((), ()))
    columns = [slice(head * DH, (head + 1) * DH) for head in range(heads)]
    keys = jnp.concatenate([k0, k1], axis=0)
    values = jnp.concatenate([v0, v1], axis=0)
    place = lax.broadcasted_iota(jnp.int32, (CL, KMAX * NB), 1)
    kept = place < live[span] * NB
    scores = [
        lax.dot_general(q_ref[:, c], keys[:, c], contract, preferred_element_type=jnp.float32)
        for c in columns
    ]
    scores = [jnp.where(kept, s / math.sqrt(DH), -1e30) for s in scores]
    weights = [jnp.exp(s - jnp.max(s, axis=-1, keepdims=True)) for s in scores]
    totals = [jnp.sum(w, axis=-1, keepdims=True) for w in weights]
    sums = [
        jnp.dot(w.astype(jnp.bfloat16), values[:, c], preferred_element_type=jnp.float32)
        for w, c in zip(weights, columns)
    ]
    for c, summed, total in zip(columns, sums, totals):
        o_ref[:, c] = (summed / total).astype(o_ref.dtype)


def attend(queries, keys, values, slots, live, capacity):
    chunks, _, parts, _, rows, width = keys.shape
    spans = live.shape[0]

    def block(entry):
        def place(c, slots, live):
            slot = slots[c * KMAX + entry]
            return (0, slot // capacity, 0, lax.rem(slot, capacity), 0, 0)

        return pl.BlockSpec((chunks, 1, parts, 1, rows, width), place)

    rows_of = pl.BlockSpec((CL, width), lambda c, slots, live: (c, 0))
    return pl.pallas_call(
        functools.partial(attend_kernel, width // DH),
        out_shape=jax.ShapeDtypeStruct(queries.shape, jnp.bfloat16),
        grid_spec=pltpu.PrefetchScalarGridSpec(
            num_scalar_prefetch=2,
            grid=(spans,),
            in_specs=[rows_of, block(0), block(1), block(0), block(1)],
            out_specs=rows_of,
        ),
        compiler_params=pltpu.CompilerParams(vmem_limit_bytes=32 * 2**20),
    )(slots, live, queries, keys, keys, values, values)


MESH = pl.DeviceIdType.MESH
TILE = 256
CHUNKS = 2


def exchange_kernel(
    capacity,
    rows_ref,
    gain_ref,
    up_ref,
    down_ref,
    final_ref,
    key_ref,
    value_ref,
    want_ref,
    keys_ref,
    values_ref,
    normed,
    hidden,
    sums,
    core_sums,
    far_sums,
    finals,
    wanted,
    outgoing,
    landed,
    key_stage,
    value_stage,
    list_send,
    list_recv,
    sum_send,
    sum_recv,
    far_send,
    far_recv,
    pick_send,
    pick_recv,
    x_send,
    x_recv,
    core_send,
    core_recv,
    diag_send,
    diag_recv,
    key_sem,
    value_sem,
):
    seq_count = want_ref.shape[0]
    features = rows_ref.shape[-1]
    chunk_rows = finals.shape[1]
    piece = outgoing.shape[1] // capacity
    tile_rows = 4 * outgoing.shape[1]
    steps = CHUNKS * seq_count
    seq, ten, enc = lax.axis_index("seq"), lax.axis_index("tensor"), lax.axis_index("enc")
    x_mate = (seq, 1 - ten, enc)
    core_mate = (seq, ten, 1 - enc)

    def peer(offset):
        return (lax.rem(seq + offset + seq_count, seq_count), ten, enc)

    barrier = pltpu.get_barrier_semaphore()
    for offset in range(1, seq_count):
        pl.semaphore_signal(barrier, inc=1, device_id=peer(offset), device_id_type=MESH)
    for mate in (x_mate, core_mate):
        pl.semaphore_signal(barrier, inc=1, device_id=mate, device_id_type=MESH)
    pl.semaphore_wait(barrier, seq_count + 1)

    def remote(src, dst, send, recv, device):
        return pltpu.make_async_remote_copy(
            src_ref=src,
            dst_ref=dst,
            send_sem=send,
            recv_sem=recv,
            device_id=device,
            device_id_type=MESH,
        )

    def list_copy(k):
        return remote(
            want_ref.at[k], wanted.at[k], list_send.at[k], list_recv.at[k], peer(-k)
        )

    for k in range(1, seq_count):
        list_copy(k).start()

    def feed_forward(order, member):
        rows = rows_ref[member].astype(jnp.float32)
        normed[...] = rms_scale(rows, gain_ref[...]).astype(jnp.bfloat16)

        @pl.loop(0, up_ref.shape[1] // TILE)
        def _(n):
            cols = pl.ds(pl.multiple_of(n * TILE, TILE), TILE)
            hidden[:, cols] = jax.nn.gelu(
                jnp.dot(normed[...], up_ref[:, cols], preferred_element_type=jnp.float32)
            ).astype(jnp.bfloat16)

        @pl.loop(0, features // TILE)
        def _(n):
            cols = pl.ds(pl.multiple_of(n * TILE, TILE), TILE)
            sums[order, :, cols] = jnp.dot(
                hidden[...], down_ref[:, cols], preferred_element_type=jnp.float32
            )

    def sum_copy(i):
        return remote(
            sums.at[2 * i], core_sums.at[i], sum_send.at[i], sum_recv.at[i], core_mate
        )

    def far_copy(c):
        span = pl.ds(c * chunk_rows, chunk_rows)
        return remote(
            sums.at[1, span], far_sums.at[c], far_send.at[c], far_recv.at[c], x_mate
        )

    feed_forward(0, 2 * (1 - ten) + 1 - enc)
    sum_copy(0).start()
    feed_forward(1, 2 * (1 - ten) + enc)
    sum_copy(0).wait_recv()
    for c in range(CHUNKS):
        span = pl.ds(c * chunk_rows, chunk_rows)
        sums[1, span, :] += core_sums[0, span, :]
        far_copy(c).start()
    feed_forward(2, 2 * ten + 1 - enc)
    sum_copy(1).start()
    feed_forward(3, 2 * ten + enc)
    sum_copy(1).wait_recv()

    def pick_copy(s, k):
        return remote(
            outgoing.at[s], landed.at[0, s], pick_send.at[s], pick_recv.at[s], peer(k)
        )

    lane = lax.broadcasted_iota(jnp.int32, (piece, chunk_rows), 1)
    row = lax.broadcasted_iota(jnp.int32, (piece, chunk_rows), 0)
    same_row = lax.rem(lane, piece) == row
    lane_block = lax.div(lane, piece)

    def pick(c, want):
        marks = [
            jnp.where(
                jnp.logical_and(want[t : t + 1, :] == lane_block, same_row), 1.0, 0.0
            ).astype(jnp.bfloat16)
            for t in range(capacity)
        ]
        return jnp.dot(
            jnp.concatenate(marks, axis=0), finals[c], preferred_element_type=jnp.float32
        ).astype(jnp.bfloat16)

    for c in range(CHUNKS):
        span = pl.ds(c * chunk_rows, chunk_rows)
        far_copy(c).wait_recv()
        encoded = rows_ref[2 * ten + enc, span, :].astype(jnp.float32) + (
            (sums[3, span, :] + core_sums[1, span, :]) + far_sums[c]
        )
        finals[c] = rms_scale(encoded, final_ref[...]).astype(jnp.bfloat16)
        landed[0, c * seq_count] = pick(c, want_ref[0])

        @pl.loop(1, seq_count)
        def _(k):
            if c == 0:
                list_copy(k).wait_recv()
            outgoing[c * seq_count + k] = pick(c, wanted[k])
            pick_copy(c * seq_count + k, k).start()

    def x_copy(s):
        return remote(landed.at[0, s], landed.at[1, s], x_send.at[s], x_recv.at[s], x_mate)

    def core_copy(s):
        return remote(
            landed.at[0, s], landed.at[2, s], core_send.at[s], core_recv.at[s], core_mate
        )

    def diag_copy(s):
        return remote(
            landed.at[1, s], landed.at[3, s], diag_send.at[s], diag_recv.at[s], core_mate
        )

    def store_copies(s):
        slot = lax.rem(s, 2)
        return (
            pltpu.make_async_copy(key_stage.at[slot], keys_ref.at[s], key_sem.at[slot]),
            pltpu.make_async_copy(value_stage.at[slot], values_ref.at[s], value_sem.at[slot]),
        )

    @pl.loop(0, steps + 2)
    def _(s):
        @pl.when(s < steps)
        def _():
            k = lax.rem(s, seq_count)

            @pl.when(k > 0)
            def _():
                pick_copy(s, k).wait_recv()

            x_copy(s).start()
            core_copy(s).start()

        @pl.when(jnp.logical_and(s >= 1, s < steps + 1))
        def _():
            x_copy(s - 1).wait_recv()
            diag_copy(s - 1).start()

        @pl.when(s >= 2)
        def _():
            done = s - 2
            core_copy(done).wait_recv()
            diag_copy(done).wait_recv()

            @pl.when(done >= 2)
            def _():
                for copy in store_copies(done - 2):
                    copy.wait()

            slot = lax.rem(done, 2)
            rows = landed[:, done].reshape(tile_rows, features)

            @pl.loop(0, key_ref.shape[1] // TILE)
            def _(n):
                cols = pl.ds(pl.multiple_of(n * TILE, TILE), TILE)
                key_stage[slot, :, cols] = jnp.dot(
                    rows, key_ref[:, cols], preferred_element_type=jnp.float32
                ).astype(jnp.bfloat16)
                value_stage[slot, :, cols] = jnp.dot(
                    rows, value_ref[:, cols], preferred_element_type=jnp.float32
                ).astype(jnp.bfloat16)

            for copy in store_copies(done):
                copy.start()

    for s in (steps - 2, steps - 1):
        for copy in store_copies(s):
            copy.wait()
    for k in range(1, seq_count):
        list_copy(k).wait_send()
    for i in range(2):
        sum_copy(i).wait_send()
    for c in range(CHUNKS):
        far_copy(c).wait_send()

    @pl.loop(0, steps)
    def _(s):
        @pl.when(lax.rem(s, seq_count) > 0)
        def _():
            pick_copy(s, lax.rem(s, seq_count)).wait_send()

        x_copy(s).wait_send()
        core_copy(s).wait_send()
        diag_copy(s).wait_send()


def exchange(rows, norm_gain, up, down, final_gain, key_weight, value_weight, want, capacity):
    group, part_rows, features = rows.shape
    seq_count = want.shape[0]
    steps = CHUNKS * seq_count
    width = key_weight.shape[1]
    chunk_rows = part_rows // CHUNKS
    piece_rows = capacity * (NB // group // CHUNKS)
    out = jax.ShapeDtypeStruct((steps, group * piece_rows, width), jnp.bfloat16)
    bf16, f32 = jnp.bfloat16, jnp.float32
    dma = pltpu.SemaphoreType.DMA
    rows_out = 2 * group * piece_rows * seq_count * CHUNKS * features * width
    return pl.pallas_call(
        functools.partial(exchange_kernel, capacity),
        out_shape=(out, out),
        in_specs=[pl.BlockSpec(memory_space=pltpu.VMEM)] * 8,
        out_specs=(pl.BlockSpec(memory_space=pl.ANY),) * 2,
        scratch_shapes=[
            pltpu.VMEM((part_rows, features), bf16),
            pltpu.VMEM((part_rows, up.shape[1]), bf16),
            pltpu.VMEM((group, part_rows, features), f32),
            pltpu.VMEM((2, part_rows, features), f32),
            pltpu.VMEM((CHUNKS, chunk_rows, features), f32),
            pltpu.VMEM((CHUNKS, chunk_rows, features), bf16),
            pltpu.VMEM(want.shape, jnp.int32),
            pltpu.VMEM((steps, piece_rows, features), bf16),
            pltpu.VMEM((group, steps, piece_rows, features), bf16),
            pltpu.VMEM((2, group * piece_rows, width), bf16),
            pltpu.VMEM((2, group * piece_rows, width), bf16),
            dma((seq_count,)),
            dma((seq_count,)),
            dma((2,)),
            dma((2,)),
            dma((CHUNKS,)),
            dma((CHUNKS,)),
            *[dma((steps,)) for _ in range(8)],
            dma((2,)),
            dma((2,)),
        ],
        compiler_params=pltpu.CompilerParams(
            collective_id=0, has_side_effects=True, vmem_limit_bytes=56 * 2**20
        ),
        cost_estimate=pl.CostEstimate(
            flops=2 * rows_out, bytes_accessed=32 * 2**20, transcendentals=0
        ),
    )(
        rows,
        norm_gain.reshape(1, -1),
        up,
        down,
        final_gain.reshape(1, -1),
        key_weight,
        value_weight,
        want,
    )


def exchanged_attention(
    neighbour_rows,
    norm_gain,
    up_weight,
    down_weight,
    final_gain,
    key_weight,
    value_weight,
    queries,
    block_lists,
    live_counts,
):
    features = neighbour_rows.shape[1]
    blocks = neighbour_rows.shape[0] // NB
    group = lax.axis_size("tensor") * lax.axis_size("enc")
    piece = NB // group // CHUNKS
    seq_count = lax.axis_size("seq")
    need_count = live_counts.shape[0] * KMAX
    capacity = (need_count + seq_count - 1) // seq_count
    width = key_weight.shape[1]
    flat_lists = block_lists.reshape(need_count)
    behind = lax.rem(lax.axis_index("seq") - flat_lists // blocks + seq_count, seq_count)
    slot_index = behind * capacity + need_ranks(behind)
    places = jnp.arange(seq_count * capacity)
    chosen = slot_index[None, :] == places[:, None]
    picked = jnp.sum(jnp.where(chosen, (flat_lists % blocks)[None, :], 0), axis=1)
    want = jnp.broadcast_to(
        picked.reshape(seq_count, capacity, 1), (seq_count, capacity, blocks * piece)
    )
    want = jnp.pad(want, ((0, 0), (0, -capacity % 8), (0, 0))).astype(jnp.int32)
    spread = jnp.transpose(
        neighbour_rows.reshape(blocks, group, CHUNKS, piece, features), (1, 2, 0, 3, 4)
    ).reshape(group, CHUNKS * blocks * piece, features)
    keys, values = exchange(
        spread,
        norm_gain,
        up_weight,
        down_weight,
        final_gain,
        key_weight,
        value_weight,
        want,
        capacity,
    )
    shape = (CHUNKS, seq_count, group, capacity, piece, width)
    return attend(
        queries, keys.reshape(shape), values.reshape(shape), slot_index, live_counts, capacity
    )


def shards(
    neighbour_rows,
    norm_gain,
    up_weight,
    down_weight,
    final_gain,
    key_weight,
    value_weight,
    queries,
    block_lists,
    live_counts,
):
    features = neighbour_rows.shape[1]
    blocks = neighbour_rows.shape[0] // NB
    group = lax.axis_size("tensor") * lax.axis_size("enc")
    part = NB // group
    seq_count = lax.axis_size("seq")
    span_count = live_counts.shape[0]
    need_count = span_count * KMAX
    capacity = (need_count + seq_count - 1) // seq_count

    flat_lists = block_lists.reshape(need_count)
    owners = flat_lists // blocks
    slot_index = owners * capacity + need_ranks(owners)
    every_list = lax.all_gather(block_lists, "seq", axis=0, tiled=True)
    every_flat = every_list.reshape(seq_count, need_count)
    every_owner = every_flat // blocks
    every_rank = need_ranks(every_owner)
    position = lax.axis_index("seq")
    slot_match = jnp.logical_and(
        every_owner[:, :, None] == position,
        every_rank[:, :, None] == jnp.arange(capacity)[None, None, :],
    )
    local_index = every_flat % blocks
    picked = jnp.sum(jnp.where(slot_match, local_index[:, :, None], 0), axis=1).reshape(-1)
    chosen = (picked[:, None] == jnp.arange(blocks)[None, :]).astype(jnp.bfloat16)

    spread = jnp.transpose(neighbour_rows.reshape(blocks, group, part, features), (1, 0, 2, 3))
    widened = spread.reshape(group * blocks * part, features).astype(jnp.float32)
    normed = rms_scale(widened, norm_gain).astype(jnp.bfloat16)
    hidden = jax.nn.gelu(jnp.dot(normed, up_weight, preferred_element_type=jnp.float32)).astype(
        jnp.bfloat16
    )
    partial_sum = jnp.dot(hidden, down_weight, preferred_element_type=jnp.float32)
    summed = lax.psum_scatter(partial_sum, GROUP, scatter_dimension=0, tiled=True)
    me = lax.axis_index("tensor") * lax.axis_size("enc") + lax.axis_index("enc")
    own = lax.dynamic_index_in_dim(spread, me, 0, keepdims=False)
    encoded = own.reshape(blocks * part, features).astype(jnp.float32) + summed
    final_rows = rms_scale(encoded, final_gain).astype(jnp.bfloat16)
    outgoing = jnp.dot(
        chosen,
        final_rows.reshape(blocks, part * features),
        preferred_element_type=jnp.float32,
    ).astype(jnp.bfloat16)
    outgoing = outgoing.reshape(seq_count, capacity * part, features)
    incoming = lax.all_to_all(outgoing, "seq", split_axis=0, concat_axis=0, tiled=True)
    gathered = lax.all_gather(incoming, GROUP, axis=0, tiled=True)
    gathered = gathered.reshape(-1, features)
    shape = (1, 1, group, seq_count * capacity, part, key_weight.shape[1])
    keys = jnp.dot(gathered, key_weight, preferred_element_type=jnp.float32).astype(jnp.bfloat16)
    values = jnp.dot(gathered, value_weight, preferred_element_type=jnp.float32).astype(
        jnp.bfloat16
    )
    return attend(queries, keys.reshape(shape), values.reshape(shape), slot_index, live_counts, seq_count * capacity)


def solution(mesh):
    placed = (
        P("seq", None),
        P(),
        P(None, GROUP),
        P(GROUP, None),
        P(),
        P(None, GROUP),
        P(None, GROUP),
        P("seq", GROUP),
        P("seq", None),
        P("seq"),
    )
    members = mesh.shape["tensor"] * mesh.shape["enc"]
    paired = mesh.shape["tensor"] == 2 and mesh.shape["enc"] == 2
    fits = paired and NB % (members * CHUNKS * 16) == 0
    return jax.shard_map(
        exchanged_attention if fits else shards, mesh=mesh, in_specs=placed, out_specs=P("seq", GROUP), check_vma=False
    )
```

```python
import functools
import math

import jax
import jax.numpy as jnp
from jax import lax
from jax.experimental import pallas as pl
from jax.experimental.pallas import tpu as pltpu
from jax.sharding import PartitionSpec as P

DH = 128
NB = 128
CL = 64
KMAX = 2
GROUP = ("tensor", "enc")


def rms_scale(rows, gain):
    mean_square = jnp.mean(rows * rows, axis=-1, keepdims=True)
    return rows * lax.rsqrt(mean_square + 1e-06) * gain


def need_ranks(owners):
    need_count = owners.shape[-1]
    order_index = jnp.arange(need_count)
    same_owner = owners[..., :, None] == owners[..., None, :]
    earlier = order_index[None, :] < order_index[:, None]
    return jnp.sum(jnp.logical_and(same_owner, earlier), axis=-1)


def attend_kernel(heads, slots, live, q_ref, k0_ref, k1_ref, v0_ref, v1_ref, o_ref):
    span = pl.program_id(0)
    width = heads * DH
    k0 = k0_ref[...].reshape(NB, width)
    k1 = k1_ref[...].reshape(NB, width)
    v0 = v0_ref[...].reshape(NB, width)
    v1 = v1_ref[...].reshape(NB, width)
    contract = (((1,), (1,)), ((), ()))
    columns = [slice(head * DH, (head + 1) * DH) for head in range(heads)]
    keys = jnp.concatenate([k0, k1], axis=0)
    values = jnp.concatenate([v0, v1], axis=0)
    place = lax.broadcasted_iota(jnp.int32, (CL, KMAX * NB), 1)
    kept = place < live[span] * NB
    scores = [
        lax.dot_general(q_ref[:, c], keys[:, c], contract, preferred_element_type=jnp.float32)
        for c in columns
    ]
    scores = [jnp.where(kept, s / math.sqrt(DH), -1e30) for s in scores]
    weights = [jnp.exp(s - jnp.max(s, axis=-1, keepdims=True)) for s in scores]
    totals = [jnp.sum(w, axis=-1, keepdims=True) for w in weights]
    sums = [
        jnp.dot(w.astype(jnp.bfloat16), values[:, c], preferred_element_type=jnp.float32)
        for w, c in zip(weights, columns)
    ]
    for c, summed, total in zip(columns, sums, totals):
        o_ref[:, c] = (summed / total).astype(o_ref.dtype)


def attend(queries, keys, values, slots, live, capacity):
    chunks, _, parts, _, rows, width = keys.shape
    spans = live.shape[0]

    def block(entry):
        def place(c, slots, live):
            slot = slots[c * KMAX + entry]
            return (0, slot // capacity, 0, lax.rem(slot, capacity), 0, 0)

        return pl.BlockSpec((chunks, 1, parts, 1, rows, width), place)

    rows_of = pl.BlockSpec((CL, width), lambda c, slots, live: (c, 0))
    return pl.pallas_call(
        functools.partial(attend_kernel, width // DH),
        out_shape=jax.ShapeDtypeStruct(queries.shape, jnp.bfloat16),
        grid_spec=pltpu.PrefetchScalarGridSpec(
            num_scalar_prefetch=2,
            grid=(spans,),
            in_specs=[rows_of, block(0), block(1), block(0), block(1)],
            out_specs=rows_of,
        ),
        compiler_params=pltpu.CompilerParams(vmem_limit_bytes=60 * 2**20),
    )(slots, live, queries, keys, keys, values, values)


MESH = pl.DeviceIdType.MESH
TILE = 256
CHUNKS = 2
STRIDE = 3
AHEAD = 3


def exchange_kernel(
    capacity,
    rows_ref,
    gain_ref,
    up_ref,
    down_ref,
    final_ref,
    key_ref,
    value_ref,
    want_ref,
    keys_ref,
    values_ref,
    normed,
    hidden,
    sums,
    core_sums,
    far_out,
    far_sums,
    finals,
    wanted,
    outgoing,
    landed,
    key_stage,
    value_stage,
    list_send,
    list_recv,
    sum_send,
    sum_recv,
    far_send,
    far_recv,
    pick_send,
    pick_recv,
    x_send,
    x_recv,
    core_send,
    core_recv,
    diag_send,
    diag_recv,
    key_sem,
    value_sem,
):
    seq_count = want_ref.shape[0]
    features = rows_ref.shape[-1]
    chunk_rows = finals.shape[1]
    piece = outgoing.shape[1] // capacity
    tile_rows = 4 * outgoing.shape[1]
    steps = CHUNKS * seq_count
    seq, ten, enc = lax.axis_index("seq"), lax.axis_index("tensor"), lax.axis_index("enc")
    x_mate = (seq, 1 - ten, enc)
    core_mate = (seq, ten, 1 - enc)

    def peer(offset):
        return (lax.rem(seq + offset + seq_count, seq_count), ten, enc)

    barrier = pltpu.get_barrier_semaphore()
    for offset in range(1, seq_count):
        pl.semaphore_signal(barrier, inc=1, device_id=peer(offset), device_id_type=MESH)
    for mate in (x_mate, core_mate):
        pl.semaphore_signal(barrier, inc=1, device_id=mate, device_id_type=MESH)
    pl.semaphore_wait(barrier, seq_count + 1)

    def remote(src, dst, send, recv, device):
        return pltpu.make_async_remote_copy(
            src_ref=src,
            dst_ref=dst,
            send_sem=send,
            recv_sem=recv,
            device_id=device,
            device_id_type=MESH,
        )

    def list_copy(k):
        return remote(
            want_ref.at[k], wanted.at[k], list_send.at[k], list_recv.at[k], peer(-k)
        )

    for k in range(1, seq_count):
        list_copy(k).start()

    def rows_of(member, c):
        rows = rows_ref[:, member, c].reshape(chunk_rows, features)
        return rows.astype(jnp.float32)

    def feed_forward(order, member):
        for c in range(CHUNKS):
            span = pl.ds(c * chunk_rows, chunk_rows)
            normed[span, :] = rms_scale(rows_of(member, c), gain_ref[...]).astype(jnp.bfloat16)

        @pl.loop(0, up_ref.shape[1] // TILE)
        def _(n):
            cols = pl.ds(pl.multiple_of(n * TILE, TILE), TILE)
            hidden[:, cols] = jax.nn.gelu(
                jnp.dot(normed[...], up_ref[:, cols], preferred_element_type=jnp.float32)
            ).astype(jnp.bfloat16)

        @pl.loop(0, features // TILE)
        def _(n):
            cols = pl.ds(pl.multiple_of(n * TILE, TILE), TILE)
            sums[order, :, cols] = jnp.dot(
                hidden[...], down_ref[:, cols], preferred_element_type=jnp.float32
            )

    def sum_copy(i):
        return remote(
            sums.at[2 * i], core_sums.at[i], sum_send.at[i], sum_recv.at[i], core_mate
        )

    def far_copy(c):
        return remote(
            far_out.at[c], far_sums.at[c], far_send.at[c], far_recv.at[c], x_mate
        )

    feed_forward(0, 2 * (1 - ten) + 1 - enc)
    sum_copy(0).start()
    feed_forward(1, 2 * (1 - ten) + enc)
    sum_copy(0).wait_recv()
    for c in range(CHUNKS):
        span = pl.ds(c * chunk_rows, chunk_rows)
        far_out[c] = (sums[1, span, :] + core_sums[0, span, :]).astype(jnp.bfloat16)
        far_copy(c).start()
    feed_forward(2, 2 * ten + 1 - enc)
    sum_copy(1).start()
    feed_forward(3, 2 * ten + enc)
    sum_copy(1).wait_recv()

    def offset_of(s):
        return lax.rem(STRIDE * lax.rem(s, seq_count), seq_count)

    def pick_copy(s):
        return remote(
            outgoing.at[s], landed.at[0, s], pick_send.at[s], pick_recv.at[s], peer(offset_of(s))
        )

    lane = lax.broadcasted_iota(jnp.int32, (piece, chunk_rows), 1)
    row = lax.broadcasted_iota(jnp.int32, (piece, chunk_rows), 0)
    same_row = lax.rem(lane, piece) == row
    lane_block = lax.div(lane, piece)

    def pick(c, want):
        marks = [
            jnp.where(
                jnp.logical_and(want[t : t + 1, :] == lane_block, same_row), 1.0, 0.0
            ).astype(jnp.bfloat16)
            for t in range(capacity)
        ]
        return jnp.dot(
            jnp.concatenate(marks, axis=0), finals[c], preferred_element_type=jnp.float32
        ).astype(jnp.bfloat16)

    def finish(c):
        span = pl.ds(c * chunk_rows, chunk_rows)
        far_copy(c).wait_recv()
        encoded = rows_of(2 * ten + enc, c) + (
            (sums[3, span, :] + core_sums[1, span, :]) + far_sums[c].astype(jnp.float32)
        )
        finals[c] = rms_scale(encoded, final_ref[...]).astype(jnp.bfloat16)
        landed[0, c * seq_count] = pick(c, want_ref[0])

    def send(s):
        k = offset_of(s)

        @pl.when(s < seq_count)
        def _():
            list_copy(k).wait_recv()

        outgoing[s] = pick(lax.div(s, seq_count), wanted[k])
        pick_copy(s).start()

    finish(0)

    @pl.loop(1, AHEAD)
    def _(s):
        send(s)

    def x_copy(s):
        return remote(landed.at[0, s], landed.at[1, s], x_send.at[s], x_recv.at[s], x_mate)

    def core_copy(s):
        return remote(
            landed.at[0, s], landed.at[2, s], core_send.at[s], core_recv.at[s], core_mate
        )

    def diag_copy(s):
        return remote(
            landed.at[1, s], landed.at[3, s], diag_send.at[s], diag_recv.at[s], core_mate
        )

    def store_copies(s):
        slot = lax.rem(s, 2)
        return (
            pltpu.make_async_copy(key_stage.at[slot], keys_ref.at[s], key_sem.at[slot]),
            pltpu.make_async_copy(value_stage.at[slot], values_ref.at[s], value_sem.at[slot]),
        )

    @pl.loop(0, steps + 2)
    def _(s):
        @pl.when(s < steps)
        def _():
            @pl.when(lax.rem(s, seq_count) > 0)
            def _():
                pick_copy(s).wait_recv()

            x_copy(s).start()
            core_copy(s).start()
            later = s + AHEAD
            for c in range(1, CHUNKS):

                @pl.when(later == c * seq_count)
                def _():
                    finish(c)

            @pl.when(jnp.logical_and(later < steps, lax.rem(later, seq_count) > 0))
            def _():
                send(later)

        @pl.when(jnp.logical_and(s >= 1, s < steps + 1))
        def _():
            x_copy(s - 1).wait_recv()
            diag_copy(s - 1).start()

        @pl.when(s >= 2)
        def _():
            done = s - 2
            core_copy(done).wait_recv()
            diag_copy(done).wait_recv()

            @pl.when(done >= 2)
            def _():
                for copy in store_copies(done - 2):
                    copy.wait()

            slot = lax.rem(done, 2)
            rows = landed[:, done].reshape(tile_rows, features)

            @pl.loop(0, key_ref.shape[1] // TILE)
            def _(n):
                cols = pl.ds(pl.multiple_of(n * TILE, TILE), TILE)
                key_stage[slot, :, cols] = jnp.dot(
                    rows, key_ref[:, cols], preferred_element_type=jnp.float32
                ).astype(jnp.bfloat16)
                value_stage[slot, :, cols] = jnp.dot(
                    rows, value_ref[:, cols], preferred_element_type=jnp.float32
                ).astype(jnp.bfloat16)

            for copy in store_copies(done):
                copy.start()

    for s in (steps - 2, steps - 1):
        for copy in store_copies(s):
            copy.wait()
    for k in range(1, seq_count):
        list_copy(k).wait_send()
    for i in range(2):
        sum_copy(i).wait_send()
    for c in range(CHUNKS):
        far_copy(c).wait_send()

    @pl.loop(0, steps)
    def _(s):
        @pl.when(lax.rem(s, seq_count) > 0)
        def _():
            pick_copy(s).wait_send()

        x_copy(s).wait_send()
        core_copy(s).wait_send()
        diag_copy(s).wait_send()


def exchange(rows, norm_gain, up, down, final_gain, key_weight, value_weight, want, capacity):
    blocks, group, _, piece, features = rows.shape
    part_rows = blocks * CHUNKS * piece
    seq_count = want.shape[0]
    steps = CHUNKS * seq_count
    width = key_weight.shape[1]
    chunk_rows = part_rows // CHUNKS
    piece_rows = capacity * (NB // group // CHUNKS)
    out = jax.ShapeDtypeStruct((steps, group * piece_rows, width), jnp.bfloat16)
    bf16, f32 = jnp.bfloat16, jnp.float32
    dma = pltpu.SemaphoreType.DMA
    rows_out = 2 * group * piece_rows * seq_count * CHUNKS * features * width
    return pl.pallas_call(
        functools.partial(exchange_kernel, capacity),
        out_shape=(out, out),
        in_specs=[pl.BlockSpec(memory_space=pltpu.VMEM)] * 8,
        out_specs=(pl.BlockSpec(memory_space=pl.ANY),) * 2,
        scratch_shapes=[
            pltpu.VMEM((part_rows, features), bf16),
            pltpu.VMEM((part_rows, up.shape[1]), bf16),
            pltpu.VMEM((group, part_rows, features), f32),
            pltpu.VMEM((2, part_rows, features), f32),
            *[pltpu.VMEM((CHUNKS, chunk_rows, features), bf16) for _ in range(3)],
            pltpu.VMEM(want.shape, jnp.int32),
            pltpu.VMEM((steps, piece_rows, features), bf16),
            pltpu.VMEM((group, steps, piece_rows, features), bf16),
            pltpu.VMEM((2, group * piece_rows, width), bf16),
            pltpu.VMEM((2, group * piece_rows, width), bf16),
            dma((seq_count,)),
            dma((seq_count,)),
            dma((2,)),
            dma((2,)),
            dma((CHUNKS,)),
            dma((CHUNKS,)),
            *[dma((steps,)) for _ in range(8)],
            dma((2,)),
            dma((2,)),
        ],
        compiler_params=pltpu.CompilerParams(
            collective_id=0, has_side_effects=True, vmem_limit_bytes=56 * 2**20
        ),
        cost_estimate=pl.CostEstimate(
            flops=2 * rows_out, bytes_accessed=32 * 2**20, transcendentals=0
        ),
    )(
        rows,
        norm_gain.reshape(1, -1),
        up,
        down,
        final_gain.reshape(1, -1),
        key_weight,
        value_weight,
        want,
    )


def exchanged_attention(
    neighbour_rows,
    norm_gain,
    up_weight,
    down_weight,
    final_gain,
    key_weight,
    value_weight,
    queries,
    block_lists,
    live_counts,
):
    features = neighbour_rows.shape[1]
    blocks = neighbour_rows.shape[0] // NB
    group = lax.axis_size("tensor") * lax.axis_size("enc")
    piece = NB // group // CHUNKS
    seq_count = lax.axis_size("seq")
    need_count = live_counts.shape[0] * KMAX
    capacity = (need_count + seq_count - 1) // seq_count
    width = key_weight.shape[1]
    flat_lists = block_lists.reshape(need_count)
    behind = lax.rem(lax.axis_index("seq") - flat_lists // blocks + seq_count, seq_count)
    rank = need_ranks(behind)
    step = lax.rem(behind * pow(STRIDE, -1, seq_count), seq_count)
    slot_index = step * capacity + rank
    want_index = behind * capacity + rank
    places = jnp.arange(seq_count * capacity)
    chosen = want_index[None, :] == places[:, None]
    picked = jnp.sum(jnp.where(chosen, (flat_lists % blocks)[None, :], 0), axis=1)
    want = jnp.broadcast_to(
        picked.reshape(seq_count, capacity, 1), (seq_count, capacity, blocks * piece)
    )
    want = jnp.pad(want, ((0, 0), (0, -capacity % 8), (0, 0))).astype(jnp.int32)
    spread = neighbour_rows.reshape(blocks, group, CHUNKS, piece, features)
    keys, values = exchange(
        spread,
        norm_gain,
        up_weight,
        down_weight,
        final_gain,
        key_weight,
        value_weight,
        want,
        capacity,
    )
    shape = (CHUNKS, seq_count, group, capacity, piece, width)
    return attend(
        queries, keys.reshape(shape), values.reshape(shape), slot_index, live_counts, capacity
    )


def shards(
    neighbour_rows,
    norm_gain,
    up_weight,
    down_weight,
    final_gain,
    key_weight,
    value_weight,
    queries,
    block_lists,
    live_counts,
):
    features = neighbour_rows.shape[1]
    blocks = neighbour_rows.shape[0] // NB
    group = lax.axis_size("tensor") * lax.axis_size("enc")
    part = NB // group
    seq_count = lax.axis_size("seq")
    span_count = live_counts.shape[0]
    need_count = span_count * KMAX
    capacity = (need_count + seq_count - 1) // seq_count

    flat_lists = block_lists.reshape(need_count)
    owners = flat_lists // blocks
    slot_index = owners * capacity + need_ranks(owners)
    every_list = lax.all_gather(block_lists, "seq", axis=0, tiled=True)
    every_flat = every_list.reshape(seq_count, need_count)
    every_owner = every_flat // blocks
    every_rank = need_ranks(every_owner)
    position = lax.axis_index("seq")
    slot_match = jnp.logical_and(
        every_owner[:, :, None] == position,
        every_rank[:, :, None] == jnp.arange(capacity)[None, None, :],
    )
    local_index = every_flat % blocks
    picked = jnp.sum(jnp.where(slot_match, local_index[:, :, None], 0), axis=1).reshape(-1)
    chosen = (picked[:, None] == jnp.arange(blocks)[None, :]).astype(jnp.bfloat16)

    spread = jnp.transpose(neighbour_rows.reshape(blocks, group, part, features), (1, 0, 2, 3))
    widened = spread.reshape(group * blocks * part, features).astype(jnp.float32)
    normed = rms_scale(widened, norm_gain).astype(jnp.bfloat16)
    hidden = jax.nn.gelu(jnp.dot(normed, up_weight, preferred_element_type=jnp.float32)).astype(
        jnp.bfloat16
    )
    partial_sum = jnp.dot(hidden, down_weight, preferred_element_type=jnp.float32)
    summed = lax.psum_scatter(partial_sum, GROUP, scatter_dimension=0, tiled=True)
    me = lax.axis_index("tensor") * lax.axis_size("enc") + lax.axis_index("enc")
    own = lax.dynamic_index_in_dim(spread, me, 0, keepdims=False)
    encoded = own.reshape(blocks * part, features).astype(jnp.float32) + summed
    final_rows = rms_scale(encoded, final_gain).astype(jnp.bfloat16)
    outgoing = jnp.dot(
        chosen,
        final_rows.reshape(blocks, part * features),
        preferred_element_type=jnp.float32,
    ).astype(jnp.bfloat16)
    outgoing = outgoing.reshape(seq_count, capacity * part, features)
    incoming = lax.all_to_all(outgoing, "seq", split_axis=0, concat_axis=0, tiled=True)
    gathered = lax.all_gather(incoming, GROUP, axis=0, tiled=True)
    gathered = gathered.reshape(-1, features)
    shape = (1, 1, group, seq_count * capacity, part, key_weight.shape[1])
    keys = jnp.dot(gathered, key_weight, preferred_element_type=jnp.float32).astype(jnp.bfloat16)
    values = jnp.dot(gathered, value_weight, preferred_element_type=jnp.float32).astype(
        jnp.bfloat16
    )
    return attend(queries, keys.reshape(shape), values.reshape(shape), slot_index, live_counts, seq_count * capacity)


def solution(mesh):
    placed = (
        P("seq", None),
        P(),
        P(None, GROUP),
        P(GROUP, None),
        P(),
        P(None, GROUP),
        P(None, GROUP),
        P("seq", GROUP),
        P("seq", None),
        P("seq"),
    )
    members = mesh.shape["tensor"] * mesh.shape["enc"]
    paired = mesh.shape["tensor"] == 2 and mesh.shape["enc"] == 2
    stepped = mesh.shape["seq"] > AHEAD and mesh.shape["seq"] % STRIDE != 0
    fits = paired and stepped and NB % (members * CHUNKS * 16) == 0
    return jax.shard_map(
        exchanged_attention if fits else shards, mesh=mesh, in_specs=placed, out_specs=P("seq", GROUP), check_vma=False
    )
```

```python
import functools
import math

import jax
import jax.numpy as jnp
from jax import lax
from jax.experimental import pallas as pl
from jax.experimental.pallas import tpu as pltpu
from jax.sharding import PartitionSpec as P

DH = 128
NB = 128
CL = 64
KMAX = 2
GROUP = ("tensor", "enc")


def rms_scale(rows, gain):
    mean_square = jnp.mean(rows * rows, axis=-1, keepdims=True)
    return rows * lax.rsqrt(mean_square + 1e-06) * gain


def need_ranks(owners):
    need_count = owners.shape[-1]
    order_index = jnp.arange(need_count)
    same_owner = owners[..., :, None] == owners[..., None, :]
    earlier = order_index[None, :] < order_index[:, None]
    return jnp.sum(jnp.logical_and(same_owner, earlier), axis=-1)


def attend_kernel(heads, slots, live, q_ref, k0_ref, k1_ref, v0_ref, v1_ref, o_ref):
    span = pl.program_id(0)
    width = heads * DH
    k0 = k0_ref[...].reshape(NB, width)
    k1 = k1_ref[...].reshape(NB, width)
    v0 = v0_ref[...].reshape(NB, width)
    v1 = v1_ref[...].reshape(NB, width)
    contract = (((1,), (1,)), ((), ()))
    columns = [slice(head * DH, (head + 1) * DH) for head in range(heads)]
    keys = jnp.concatenate([k0, k1], axis=0)
    values = jnp.concatenate([v0, v1], axis=0)
    place = lax.broadcasted_iota(jnp.int32, (CL, KMAX * NB), 1)
    kept = place < live[span] * NB
    scores = [
        lax.dot_general(q_ref[:, c], keys[:, c], contract, preferred_element_type=jnp.float32)
        for c in columns
    ]
    scores = [jnp.where(kept, s / math.sqrt(DH), -1e30) for s in scores]
    weights = [jnp.exp(s - jnp.max(s, axis=-1, keepdims=True)) for s in scores]
    totals = [jnp.sum(w, axis=-1, keepdims=True) for w in weights]
    sums = [
        jnp.dot(w.astype(jnp.bfloat16), values[:, c], preferred_element_type=jnp.float32)
        for w, c in zip(weights, columns)
    ]
    for c, summed, total in zip(columns, sums, totals):
        o_ref[:, c] = (summed / total).astype(o_ref.dtype)


def attend(queries, keys, values, slots, live, capacity):
    chunks, _, parts, _, rows, width = keys.shape
    spans = live.shape[0]

    def block(entry):
        def place(c, slots, live):
            slot = slots[c * KMAX + entry]
            return (0, slot // capacity, 0, lax.rem(slot, capacity), 0, 0)

        return pl.BlockSpec((chunks, 1, parts, 1, rows, width), place)

    rows_of = pl.BlockSpec((CL, width), lambda c, slots, live: (c, 0))
    return pl.pallas_call(
        functools.partial(attend_kernel, width // DH),
        out_shape=jax.ShapeDtypeStruct(queries.shape, jnp.bfloat16),
        grid_spec=pltpu.PrefetchScalarGridSpec(
            num_scalar_prefetch=2,
            grid=(spans,),
            in_specs=[rows_of, block(0), block(1), block(0), block(1)],
            out_specs=rows_of,
        ),
        compiler_params=pltpu.CompilerParams(vmem_limit_bytes=60 * 2**20),
    )(slots, live, queries, keys, keys, values, values)


MESH = pl.DeviceIdType.MESH
TILE = 1024
CHUNKS = 2
STRIDE = 3
AHEAD = 3


def exchange_kernel(
    capacity,
    rows_ref,
    gain_ref,
    up_ref,
    down_ref,
    final_ref,
    key_ref,
    value_ref,
    want_ref,
    keys_ref,
    values_ref,
    normed,
    hidden,
    sums,
    core_sums,
    far_out,
    far_sums,
    finals,
    wanted,
    outgoing,
    landed,
    key_stage,
    value_stage,
    list_send,
    list_recv,
    sum_send,
    sum_recv,
    far_send,
    far_recv,
    pick_send,
    pick_recv,
    x_send,
    x_recv,
    core_send,
    core_recv,
    diag_send,
    diag_recv,
    key_sem,
    value_sem,
):
    seq_count = want_ref.shape[0]
    features = rows_ref.shape[-1]
    chunk_rows = finals.shape[1]
    piece = outgoing.shape[1] // capacity
    tile_rows = 4 * outgoing.shape[1]
    steps = CHUNKS * seq_count
    seq, ten, enc = lax.axis_index("seq"), lax.axis_index("tensor"), lax.axis_index("enc")
    x_mate = (seq, 1 - ten, enc)
    core_mate = (seq, ten, 1 - enc)

    def peer(offset):
        return (lax.rem(seq + offset + seq_count, seq_count), ten, enc)

    barrier = pltpu.get_barrier_semaphore()
    for offset in range(1, seq_count):
        pl.semaphore_signal(barrier, inc=1, device_id=peer(offset), device_id_type=MESH)
    for mate in (x_mate, core_mate):
        pl.semaphore_signal(barrier, inc=1, device_id=mate, device_id_type=MESH)
    pl.semaphore_wait(barrier, seq_count + 1)

    def remote(src, dst, send, recv, device):
        return pltpu.make_async_remote_copy(
            src_ref=src,
            dst_ref=dst,
            send_sem=send,
            recv_sem=recv,
            device_id=device,
            device_id_type=MESH,
        )

    def list_copy(k):
        return remote(
            want_ref.at[k], wanted.at[k], list_send.at[k], list_recv.at[k], peer(-k)
        )

    for k in range(1, seq_count):
        list_copy(k).start()

    def rows_of(member, c):
        rows = rows_ref[:, member, c].reshape(chunk_rows, features)
        return rows.astype(jnp.float32)

    def feed_forward(order, member):
        for c in range(CHUNKS):
            span = pl.ds(c * chunk_rows, chunk_rows)
            normed[span, :] = rms_scale(rows_of(member, c), gain_ref[...]).astype(jnp.bfloat16)

        @pl.loop(0, up_ref.shape[1] // TILE)
        def _(n):
            cols = pl.ds(pl.multiple_of(n * TILE, TILE), TILE)
            hidden[:, cols] = jax.nn.gelu(
                jnp.dot(normed[...], up_ref[:, cols], preferred_element_type=jnp.float32)
            ).astype(jnp.bfloat16)

        @pl.loop(0, features // TILE)
        def _(n):
            cols = pl.ds(pl.multiple_of(n * TILE, TILE), TILE)
            sums[order, :, cols] = jnp.dot(
                hidden[...], down_ref[:, cols], preferred_element_type=jnp.float32
            )

    def sum_copy(i):
        return remote(
            sums.at[2 * i], core_sums.at[i], sum_send.at[i], sum_recv.at[i], core_mate
        )

    def far_copy(c):
        return remote(
            far_out.at[c], far_sums.at[c], far_send.at[c], far_recv.at[c], x_mate
        )

    feed_forward(0, 2 * (1 - ten) + 1 - enc)
    sum_copy(0).start()
    feed_forward(1, 2 * (1 - ten) + enc)
    sum_copy(0).wait_recv()
    for c in range(CHUNKS):
        span = pl.ds(c * chunk_rows, chunk_rows)
        far_out[c] = (sums[1, span, :] + core_sums[0, span, :]).astype(jnp.bfloat16)
        far_copy(c).start()
    feed_forward(2, 2 * ten + 1 - enc)
    sum_copy(1).start()
    feed_forward(3, 2 * ten + enc)
    sum_copy(1).wait_recv()

    def offset_of(s):
        return lax.rem(STRIDE * lax.rem(s, seq_count), seq_count)

    def pick_copy(s):
        return remote(
            outgoing.at[s], landed.at[0, s], pick_send.at[s], pick_recv.at[s], peer(offset_of(s))
        )

    lane = lax.broadcasted_iota(jnp.int32, (piece, chunk_rows), 1)
    row = lax.broadcasted_iota(jnp.int32, (piece, chunk_rows), 0)
    same_row = lax.rem(lane, piece) == row
    lane_block = lax.div(lane, piece)

    def pick(c, want):
        marks = [
            jnp.where(
                jnp.logical_and(want[t : t + 1, :] == lane_block, same_row), 1.0, 0.0
            ).astype(jnp.bfloat16)
            for t in range(capacity)
        ]
        return jnp.dot(
            jnp.concatenate(marks, axis=0), finals[c], preferred_element_type=jnp.float32
        ).astype(jnp.bfloat16)

    def finish(c):
        span = pl.ds(c * chunk_rows, chunk_rows)
        far_copy(c).wait_recv()
        encoded = rows_of(2 * ten + enc, c) + (
            (sums[3, span, :] + core_sums[1, span, :]) + far_sums[c].astype(jnp.float32)
        )
        finals[c] = rms_scale(encoded, final_ref[...]).astype(jnp.bfloat16)
        landed[0, c * seq_count] = pick(c, want_ref[0])

    def send(s):
        k = offset_of(s)

        @pl.when(s < seq_count)
        def _():
            list_copy(k).wait_recv()

        outgoing[s] = pick(lax.div(s, seq_count), wanted[k])
        pick_copy(s).start()

    finish(0)

    @pl.loop(1, AHEAD)
    def _(s):
        send(s)

    def x_copy(s):
        return remote(landed.at[0, s], landed.at[1, s], x_send.at[s], x_recv.at[s], x_mate)

    def core_copy(s):
        return remote(
            landed.at[0, s], landed.at[2, s], core_send.at[s], core_recv.at[s], core_mate
        )

    def diag_copy(s):
        return remote(
            landed.at[1, s], landed.at[3, s], diag_send.at[s], diag_recv.at[s], core_mate
        )

    def store_copies(s):
        slot = lax.rem(s, 2)
        return (
            pltpu.make_async_copy(key_stage.at[slot], keys_ref.at[s], key_sem.at[slot]),
            pltpu.make_async_copy(value_stage.at[slot], values_ref.at[s], value_sem.at[slot]),
        )

    @pl.loop(0, steps + 2)
    def _(s):
        @pl.when(s < steps)
        def _():
            @pl.when(lax.rem(s, seq_count) > 0)
            def _():
                pick_copy(s).wait_recv()

            x_copy(s).start()
            core_copy(s).start()
            later = s + AHEAD
            for c in range(1, CHUNKS):

                @pl.when(later == c * seq_count)
                def _():
                    finish(c)

            @pl.when(jnp.logical_and(later < steps, lax.rem(later, seq_count) > 0))
            def _():
                send(later)

        @pl.when(jnp.logical_and(s >= 1, s < steps + 1))
        def _():
            x_copy(s - 1).wait_recv()
            diag_copy(s - 1).start()

        @pl.when(s >= 2)
        def _():
            done = s - 2
            core_copy(done).wait_recv()
            diag_copy(done).wait_recv()

            @pl.when(done >= 2)
            def _():
                for copy in store_copies(done - 2):
                    copy.wait()

            slot = lax.rem(done, 2)
            rows = landed[:, done].reshape(tile_rows, features)

            @pl.loop(0, key_ref.shape[1] // TILE)
            def _(n):
                cols = pl.ds(pl.multiple_of(n * TILE, TILE), TILE)
                key_stage[slot, :, cols] = jnp.dot(
                    rows, key_ref[:, cols], preferred_element_type=jnp.float32
                ).astype(jnp.bfloat16)
                value_stage[slot, :, cols] = jnp.dot(
                    rows, value_ref[:, cols], preferred_element_type=jnp.float32
                ).astype(jnp.bfloat16)

            for copy in store_copies(done):
                copy.start()

    for s in (steps - 2, steps - 1):
        for copy in store_copies(s):
            copy.wait()
    for k in range(1, seq_count):
        list_copy(k).wait_send()
    for i in range(2):
        sum_copy(i).wait_send()
    for c in range(CHUNKS):
        far_copy(c).wait_send()

    @pl.loop(0, steps)
    def _(s):
        @pl.when(lax.rem(s, seq_count) > 0)
        def _():
            pick_copy(s).wait_send()

        x_copy(s).wait_send()
        core_copy(s).wait_send()
        diag_copy(s).wait_send()


def exchange(rows, norm_gain, up, down, final_gain, key_weight, value_weight, want, capacity):
    blocks, group, _, piece, features = rows.shape
    part_rows = blocks * CHUNKS * piece
    seq_count = want.shape[0]
    steps = CHUNKS * seq_count
    width = key_weight.shape[1]
    chunk_rows = part_rows // CHUNKS
    piece_rows = capacity * (NB // group // CHUNKS)
    out = jax.ShapeDtypeStruct((steps, group * piece_rows, width), jnp.bfloat16)
    bf16, f32 = jnp.bfloat16, jnp.float32
    dma = pltpu.SemaphoreType.DMA
    rows_out = 2 * group * piece_rows * seq_count * CHUNKS * features * width
    return pl.pallas_call(
        functools.partial(exchange_kernel, capacity),
        out_shape=(out, out),
        in_specs=[pl.BlockSpec(memory_space=pltpu.VMEM)] * 8,
        out_specs=(pl.BlockSpec(memory_space=pl.ANY),) * 2,
        scratch_shapes=[
            pltpu.VMEM((part_rows, features), bf16),
            pltpu.VMEM((part_rows, up.shape[1]), bf16),
            pltpu.VMEM((group, part_rows, features), f32),
            pltpu.VMEM((2, part_rows, features), f32),
            *[pltpu.VMEM((CHUNKS, chunk_rows, features), bf16) for _ in range(3)],
            pltpu.VMEM(want.shape, jnp.int32),
            pltpu.VMEM((steps, piece_rows, features), bf16),
            pltpu.VMEM((group, steps, piece_rows, features), bf16),
            pltpu.VMEM((2, group * piece_rows, width), bf16),
            pltpu.VMEM((2, group * piece_rows, width), bf16),
            dma((seq_count,)),
            dma((seq_count,)),
            dma((2,)),
            dma((2,)),
            dma((CHUNKS,)),
            dma((CHUNKS,)),
            *[dma((steps,)) for _ in range(8)],
            dma((2,)),
            dma((2,)),
        ],
        compiler_params=pltpu.CompilerParams(
            collective_id=0, has_side_effects=True, vmem_limit_bytes=56 * 2**20
        ),
        cost_estimate=pl.CostEstimate(
            flops=2 * rows_out, bytes_accessed=32 * 2**20, transcendentals=0
        ),
    )(
        rows,
        norm_gain.reshape(1, -1),
        up,
        down,
        final_gain.reshape(1, -1),
        key_weight,
        value_weight,
        want,
    )


def exchanged_attention(
    neighbour_rows,
    norm_gain,
    up_weight,
    down_weight,
    final_gain,
    key_weight,
    value_weight,
    queries,
    block_lists,
    live_counts,
):
    features = neighbour_rows.shape[1]
    blocks = neighbour_rows.shape[0] // NB
    group = lax.axis_size("tensor") * lax.axis_size("enc")
    piece = NB // group // CHUNKS
    seq_count = lax.axis_size("seq")
    need_count = live_counts.shape[0] * KMAX
    capacity = (need_count + seq_count - 1) // seq_count
    width = key_weight.shape[1]
    flat_lists = block_lists.reshape(need_count)
    behind = lax.rem(lax.axis_index("seq") - flat_lists // blocks + seq_count, seq_count)
    rank = need_ranks(behind)
    step = lax.rem(behind * pow(STRIDE, -1, seq_count), seq_count)
    slot_index = step * capacity + rank
    want_index = behind * capacity + rank
    places = jnp.arange(seq_count * capacity)
    chosen = want_index[None, :] == places[:, None]
    picked = jnp.sum(jnp.where(chosen, (flat_lists % blocks)[None, :], 0), axis=1)
    want = jnp.broadcast_to(
        picked.reshape(seq_count, capacity, 1), (seq_count, capacity, blocks * piece)
    )
    want = jnp.pad(want, ((0, 0), (0, -capacity % 8), (0, 0))).astype(jnp.int32)
    spread = neighbour_rows.reshape(blocks, group, CHUNKS, piece, features)
    keys, values = exchange(
        spread,
        norm_gain,
        up_weight,
        down_weight,
        final_gain,
        key_weight,
        value_weight,
        want,
        capacity,
    )
    shape = (CHUNKS, seq_count, group, capacity, piece, width)
    return attend(
        queries, keys.reshape(shape), values.reshape(shape), slot_index, live_counts, capacity
    )


def shards(
    neighbour_rows,
    norm_gain,
    up_weight,
    down_weight,
    final_gain,
    key_weight,
    value_weight,
    queries,
    block_lists,
    live_counts,
):
    features = neighbour_rows.shape[1]
    blocks = neighbour_rows.shape[0] // NB
    group = lax.axis_size("tensor") * lax.axis_size("enc")
    part = NB // group
    seq_count = lax.axis_size("seq")
    span_count = live_counts.shape[0]
    need_count = span_count * KMAX
    capacity = (need_count + seq_count - 1) // seq_count

    flat_lists = block_lists.reshape(need_count)
    owners = flat_lists // blocks
    slot_index = owners * capacity + need_ranks(owners)
    every_list = lax.all_gather(block_lists, "seq", axis=0, tiled=True)
    every_flat = every_list.reshape(seq_count, need_count)
    every_owner = every_flat // blocks
    every_rank = need_ranks(every_owner)
    position = lax.axis_index("seq")
    slot_match = jnp.logical_and(
        every_owner[:, :, None] == position,
        every_rank[:, :, None] == jnp.arange(capacity)[None, None, :],
    )
    local_index = every_flat % blocks
    picked = jnp.sum(jnp.where(slot_match, local_index[:, :, None], 0), axis=1).reshape(-1)
    chosen = (picked[:, None] == jnp.arange(blocks)[None, :]).astype(jnp.bfloat16)

    spread = jnp.transpose(neighbour_rows.reshape(blocks, group, part, features), (1, 0, 2, 3))
    widened = spread.reshape(group * blocks * part, features).astype(jnp.float32)
    normed = rms_scale(widened, norm_gain).astype(jnp.bfloat16)
    hidden = jax.nn.gelu(jnp.dot(normed, up_weight, preferred_element_type=jnp.float32)).astype(
        jnp.bfloat16
    )
    partial_sum = jnp.dot(hidden, down_weight, preferred_element_type=jnp.float32)
    summed = lax.psum_scatter(partial_sum, GROUP, scatter_dimension=0, tiled=True)
    me = lax.axis_index("tensor") * lax.axis_size("enc") + lax.axis_index("enc")
    own = lax.dynamic_index_in_dim(spread, me, 0, keepdims=False)
    encoded = own.reshape(blocks * part, features).astype(jnp.float32) + summed
    final_rows = rms_scale(encoded, final_gain).astype(jnp.bfloat16)
    outgoing = jnp.dot(
        chosen,
        final_rows.reshape(blocks, part * features),
        preferred_element_type=jnp.float32,
    ).astype(jnp.bfloat16)
    outgoing = outgoing.reshape(seq_count, capacity * part, features)
    incoming = lax.all_to_all(outgoing, "seq", split_axis=0, concat_axis=0, tiled=True)
    gathered = lax.all_gather(incoming, GROUP, axis=0, tiled=True)
    gathered = gathered.reshape(-1, features)
    shape = (1, 1, group, seq_count * capacity, part, key_weight.shape[1])
    keys = jnp.dot(gathered, key_weight, preferred_element_type=jnp.float32).astype(jnp.bfloat16)
    values = jnp.dot(gathered, value_weight, preferred_element_type=jnp.float32).astype(
        jnp.bfloat16
    )
    return attend(queries, keys.reshape(shape), values.reshape(shape), slot_index, live_counts, seq_count * capacity)


def solution(mesh):
    placed = (
        P("seq", None),
        P(),
        P(None, GROUP),
        P(GROUP, None),
        P(),
        P(None, GROUP),
        P(None, GROUP),
        P("seq", GROUP),
        P("seq", None),
        P("seq"),
    )
    members = mesh.shape["tensor"] * mesh.shape["enc"]
    paired = mesh.shape["tensor"] == 2 and mesh.shape["enc"] == 2
    stepped = mesh.shape["seq"] > AHEAD and mesh.shape["seq"] % STRIDE != 0
    fits = paired and stepped and NB % (members * CHUNKS * 16) == 0
    return jax.shard_map(
        exchanged_attention if fits else shards, mesh=mesh, in_specs=placed, out_specs=P("seq", GROUP), check_vma=False
    )
```
